32 devices in a mesh: grp: 2 (over y), dp: 4 (over z), mp: 4 (over x, core).
Axes of the slice: x: 2, y: 2, z: 4, core: 2. Of those that a mesh axis runs over, the one named last changes fastest.
Arguments:
- tokens: bfloat16 [12288, 4096], P(('grp', 'dp'), 'mp'), parts along dimension 0, may hold values from -6 to 6
- out_grad: bfloat16 [12288, 11008], P(('grp', 'dp'), 'mp'), parts along dimension 0, may hold values from -0.109375 to 0.109375
- subspace_basis: bfloat16 [4096, 512], P('mp'), may hold values from -0.09375 to 0.09375
- weights: bfloat16 [4, 2752, 4096], P('mp', 'dp'), may hold values from -0.09375 to 0.09375
- moment_first: float32 [4, 5504, 512], P('mp', ('grp', 'dp')), parts along dimension 1, may hold values from -6 to 6
- moment_second: float32 [4, 5504, 512], P('mp', ('grp', 'dp')), parts along dimension 1, may hold values from 0.01 to 2
Outputs:
- new_weights: bfloat16 [4, 5504, 4096], P(None, ('grp', 'dp')), parts along dimension 1
- first_moment: float32 [4, 5504, 512], P('mp', ('grp', 'dp')), parts along dimension 1
- second_moment: float32 [4, 5504, 512], P('mp', ('grp', 'dp')), parts along dimension 1
The draws below stay inside these ranges and needn't reach their ends.
There are 2 independent parts, one for each index of `grp`. The reference program is written for one: setup_inputs(seed, part) draws one part's arguments, and reference() takes and returns one part's arrays. A program takes and returns all parts, laid end to end along the dimension named above; an argument that names none is the same for every part. Nothing has to cross between parts.
All inputs are finite; a program needn't handle non-finite values.
Results may differ from the reference program's by a relative error of at most 0.004.
Values may be sent and summed in bfloat16 or wider, within the bound.
A program may use at most 192 MiB of HBM per device.

```python
import math
import jax
import jax.numpy as jnp

D = 4096
F = 11008
R = 512
TOKENS = 6144
N_MP = 4


def strengthened(drawn, rng, source, target, blocks, factor):
    def block_of(dim):
        return (jnp.arange(drawn.shape[dim]) // (drawn.shape[dim] // blocks)).reshape((-1,) + (1,) * (drawn.ndim - 1 - dim))

    one_side = jax.random.permutation(rng, blocks)[block_of(target)]
    second = (block_of(target) + blocks // 2) % blocks
    return jnp.where((block_of(source) == one_side) | (block_of(source) == second), factor * drawn, drawn)


def levels(rng, shape, shards, least, high):
    level, own = 1.0, jax.random.fold_in(rng, 6)
    for position, blocks in shards:
        steps = jnp.exp(jax.random.uniform(jax.random.fold_in(own, position), (blocks,), jnp.float32, least / len(shards), high / len(shards)))
        level = level * jnp.repeat(steps, shape[position] // blocks).reshape([-1 if axis == position else 1 for axis in range(len(shape))])
    return level


def centred(key, shape, deviation, bound, shards=(), kind=jnp.bfloat16):
    entries = jax.random.normal(key, shape, jnp.float32) * deviation
    if len(shards) > 0:
        entries = levels(key, shape, shards, -0.22, 0.18) * entries
    return jnp.clip(entries, min=-bound, max=bound).astype(kind)


def bell_draw_with(own_key, dims, spread, bound, pieces, heavy, dtype=jnp.bfloat16):
    entries = spread * jax.random.normal(own_key, dims, jnp.float32)
    if pieces:
        entries = entries * levels(own_key, dims, pieces, -0.22, 0.18)
    return jnp.clip(strengthened(entries, jax.random.fold_in(own_key, 3), *heavy), -bound, bound).astype(dtype)


def setup_inputs(seed: int = 0, part: int = 0) -> dict:
    key_list = jax.random.split(jax.random.key(seed), 7)
    own_keys = jax.random.split(jax.random.fold_in(key_list[6], part), 7)
    tokens = centred(own_keys[0], (TOKENS, D), 1.0, 6.0, ((0, 4), (1, 4)))
    out_grad = bell_draw_with(own_keys[1], (TOKENS, F), TOKENS ** -0.5, 0.109375, ((0, 4), (1, 4)), (0, 1, 4, 2.0))
    subspace_basis = centred(key_list[2], (D, R), D ** -0.5, 0.09375, ((0, 4),))
    weights = centred(key_list[3], (N_MP, F // N_MP, D), D ** -0.5, 0.09375, ((0, 4), (1, 4)))
    moment_first = centred(own_keys[4], (N_MP, F // N_MP, R), 1.0, 6.0, ((0, 4), (1, 4)), jnp.float32)
    moment_second = jnp.clip(jnp.exp(math.log(2.0) - 5.2983174 * jax.random.uniform(own_keys[5], (N_MP, F // N_MP, R), jnp.float32) ** levels(own_keys[5], (N_MP, F // N_MP, R), ((0, 4), (1, 4)), -0.2, 0.2)), 0.01, 2.0)
    return dict(tokens=tokens, out_grad=out_grad, subspace_basis=subspace_basis, weights=weights, moment_first=moment_first, moment_second=moment_second)


beta_one = 0.9
beta_two = 0.999
correction_one = 1.0 - 0.9 ** 10
correction_two = 1.0 - 0.999 ** 10
epsilon = 1e-08
step_size = 0.02

def reference(tokens, out_grad, subspace_basis, weights, moment_first, moment_second):
    projected = jnp.dot(tokens, subspace_basis, preferred_element_type=jnp.float32).astype(jnp.bfloat16)
    subspace_grad = jnp.dot(out_grad.T, projected, preferred_element_type=jnp.float32)
    subspace_grad = subspace_grad.reshape(N_MP, F // N_MP, R)
    first_moment = beta_one * moment_first + (1.0 - beta_one) * subspace_grad
    second_moment = beta_two * moment_second + (1.0 - beta_two) * subspace_grad * subspace_grad
    direction = (first_moment / correction_one / (jnp.sqrt(second_moment / correction_two) + epsilon)).astype(jnp.bfloat16)
    weight_delta = jnp.dot(direction.reshape(F, R), subspace_basis.T, preferred_element_type=jnp.float32)
    weight_delta = weight_delta.reshape(N_MP, F // N_MP, D)
    new_weights = (weights.astype(jnp.float32) - step_size * weight_delta).astype(jnp.bfloat16)
    return (new_weights, first_moment, second_moment)
```

```python
import functools

import jax
import jax.numpy as jnp
from jax import lax
from jax.experimental import pallas as pl
from jax.experimental.pallas import tpu as pltpu
from jax.sharding import PartitionSpec as P

beta_one = 0.9
beta_two = 0.999
correction_one = 1.0 - 0.9**10
correction_two = 1.0 - 0.999**10
epsilon = 1e-08
step_size = 0.02

MESH = pl.DeviceIdType.MESH
bf16 = jnp.bfloat16
f32 = jnp.float32

RC = 2
WC = 8


def exchange_kernel(
    n_dp,
    tokens, out_grad, basis, weights, moment_one, moment_two,
    first_out, second_out, dirs, bases, walls,
    tok_v, bas_v, og_v, p_own, p_send, p_recv, s_send, s_recv, proj,
    g_send, g_recv, m_one, m_two, direction,
    load_sem, store_sem,
    pc_s, pc_r, px_s, px_r, pf_s, pf_r, rs_s, rs_r,
    dc_s, dc_r, dx_s, dx_r, df_s, df_r,
    bc_s, bc_r, bx_s, bx_r, by_s, by_r, bf_s, bf_r, bg_s, bg_r,
    wc_s, wc_r, wx_s, wx_r, wy_s, wy_r, wf_s, wf_r, wg_s, wg_r,
):
    grp = lax.axis_index("grp")
    dp = lax.axis_index("dp")
    mp = lax.axis_index("mp")
    core = mp % 2
    mate = mp + 1 - 2 * core
    across = mp + 2 - 4 * (mp // 2)
    to_core = {"mp": mate}
    to_x = {"mp": across}
    to_y = {"grp": 1 - grp}

    tokens_own, depth = tokens.shape
    half = tokens_own // 2
    rank = basis.shape[1]
    rc = rank // RC
    hidden = weights.shape[1]
    wide = weights.shape[2]
    wh = wide // 2
    wc = wh // WC
    bh = depth // 2

    def remote(src, dst, ss, rs, where):
        return pltpu.make_async_remote_copy(
            src_ref=src, dst_ref=dst, send_sem=ss, recv_sem=rs,
            device_id=where, device_id_type=MESH,
        )

    loads = [
        pltpu.make_async_copy(src, dst, load_sem.at[i])
        for i, (src, dst) in enumerate(
            [(tokens, tok_v), (basis, bas_v), (out_grad, og_v),
             (moment_one, m_one), (moment_two, m_two)]
        )
    ]
    loads[1].start()
    loads[0].start()
    loads[2].start()

    barrier = pltpu.get_barrier_semaphore()
    for where in (to_core, to_x, to_y):
        pl.semaphore_signal(barrier, inc=1, device_id=where, device_id_type=MESH)
    for d in range(1, n_dp):
        pl.semaphore_signal(
            barrier, inc=1, device_id={"dp": (dp + d) % n_dp}, device_id_type=MESH
        )
    pl.semaphore_wait(barrier, 3 + n_dp - 1)

    def w_cols(side, k):
        return pl.ds(side * wh + k * wc, wc)

    def w_x(k):
        return remote(weights.at[0, :, w_cols(grp, k)], walls.at[mp, :, w_cols(grp, k)],
                      wx_s.at[k], wx_r.at[k], to_x)

    def w_y(k):
        view = walls.at[across, :, w_cols(grp, k)]
        return remote(view, view, wy_s.at[k], wy_r.at[k], to_y)

    def w_f(k):
        view = walls.at[across, :, w_cols(grp, k)]
        return remote(view, view, wf_s.at[k], wf_r.at[k], to_core)

    def w_g(k):
        view = walls.at[across, :, w_cols(1 - grp, k)]
        return remote(view, view, wg_s.at[k], wg_r.at[k], to_core)

    w_x(0).start()

    def project(r, row, dst):
        def body(i, _):
            at = pl.multiple_of(row + i * 256, 256)
            dst[pl.ds(pl.multiple_of(i * 256, 256), 256), :] = jnp.dot(
                tok_v[pl.ds(at, 256), :], bas_v[:, r * rc:(r + 1) * rc],
                preferred_element_type=f32,
            ).astype(dst.dtype)
            return 0
        lax.fori_loop(0, half // 256, body, 0)

    def pc(r):
        return remote(p_send.at[r], p_recv.at[r], pc_s.at[r], pc_r.at[r], to_core)

    def px(r):
        return remote(s_send.at[r], s_recv.at[r], px_s.at[r], px_r.at[r], to_x)

    def pf(r):
        view = proj.at[r, pl.ds(core * half, half), :]
        return remote(view, view, pf_s.at[r], pf_r.at[r], to_core)

    loads[1].wait()
    loads[0].wait()
    for r in range(RC):
        project(r, (1 - core) * half, p_send.at[r])
        pc(r).start()
        project(r, core * half, p_own)
        pc(r).wait_recv()
        s_send[r] = (p_own[...] + p_recv[r].astype(f32)).astype(bf16)
        px(r).start()

    loads[3].start()
    loads[4].start()

    own_w = pltpu.make_async_copy(weights.at[0], walls.at[mp], store_sem.at[2])
    own_w.start()
    w_core = remote(weights.at[0], walls.at[mp], wc_s.at[0], wc_r.at[0], to_core)
    w_core.start()
    own_b = pltpu.make_async_copy(basis, bases.at[mp], store_sem.at[3])
    own_b.start()
    b_core = remote(basis, bases.at[mp], bc_s.at[0], bc_r.at[0], to_core)
    b_core.start()
    rows_mine = pl.ds(grp * bh, bh)
    rows_other = pl.ds((1 - grp) * bh, bh)
    b_x = remote(basis.at[rows_mine, :], bases.at[mp, rows_mine, :], bx_s.at[0], bx_r.at[0], to_x)
    b_view = bases.at[across, rows_mine, :]
    b_y = remote(b_view, b_view, by_s.at[0], by_r.at[0], to_y)
    b_f = remote(b_view, b_view, bf_s.at[0], bf_r.at[0], to_core)
    b_view_other = bases.at[across, rows_other, :]
    b_g = remote(b_view_other, b_view_other, bg_s.at[0], bg_r.at[0], to_core)

    def rs(r, d):
        to = (dp + d) % n_dp
        return remote(g_send.at[r, pl.ds(to * hidden, hidden), :], g_recv.at[d - 1, r],
                      rs_s.at[r, d - 1], rs_r.at[r, d - 1], {"dp": to})

    width = out_grad.shape[1]
    tile = 256
    full = width // tile

    def gradient(r, at, size):
        g_send[r, pl.ds(at, size), :] = lax.dot_general(
            og_v[:, pl.ds(at, size)], proj[r], (((0,), (0,)), ((), ())),
            preferred_element_type=f32,
        ).astype(bf16)

    for r in range(RC):
        px(r).wait_recv()
        if r == RC - 1:
            for k in range(1, WC):
                w_x(k).start()
            b_x.start()
        proj[r, pl.ds(core * half, half), :] = (
            s_send[r].astype(f32) + s_recv[r].astype(f32)
        ).astype(bf16)
        pf(r).start()
        if r == 0:
            loads[2].wait()
        pf(r).wait_recv()

        def body(i, _, r=r):
            gradient(r, pl.multiple_of(i * tile, tile), tile)
            return 0
        lax.fori_loop(0, full, body, 0)
        if width % tile:
            gradient(r, full * tile, width % tile)
        for d in range(n_dp - 1, 0, -1):
            rs(r, d).start()

    def d_c(r):
        return remote(direction.at[r], dirs.at[mp, :, pl.ds(r * rc, rc)],
                      dc_s.at[r], dc_r.at[r], to_core)

    def d_x(r):
        return remote(direction.at[r], dirs.at[mp, :, pl.ds(r * rc, rc)],
                      dx_s.at[r], dx_r.at[r], to_x)

    def d_f(r):
        view = dirs.at[across, :, pl.ds(r * rc, rc)]
        return remote(view, view, df_s.at[r], df_r.at[r], to_core)

    def d_own(r):
        return pltpu.make_async_copy(
            direction.at[r], dirs.at[mp, :, pl.ds(r * rc, rc)], store_sem.at[4 + r])

    def adam(r):
        for d in range(1, n_dp):
            rs(r, d).wait_recv()
        cols = slice(r * rc, (r + 1) * rc)

        def body(i, _):
            at = pl.multiple_of(i * 16, 16)
            own = pl.multiple_of(dp * hidden + i * 16, 16)
            total = g_send[r, pl.ds(own, 16), :].astype(f32)
            for d in range(n_dp - 1):
                total = total + g_recv[d, r, pl.ds(at, 16), :].astype(f32)
            first = beta_one * m_one[0, pl.ds(at, 16), cols] + (1.0 - beta_one) * total
            second = beta_two * m_two[0, pl.ds(at, 16), cols] + (1.0 - beta_two) * total * total
            m_one[0, pl.ds(at, 16), cols] = first
            m_two[0, pl.ds(at, 16), cols] = second
            direction[r, pl.ds(at, 16), :] = (
                first / correction_one / (jnp.sqrt(second / correction_two) + epsilon)
            ).astype(bf16)
            return 0
        lax.fori_loop(0, hidden // 16, body, 0)
        d_x(r).start()
        d_c(r).start()
        d_own(r).start()

    def forward(k):
        w_x(k).wait_recv()
        w_y(k).start()
        w_f(k).start()

    loads[3].wait()
    loads[4].wait()
    for k in range(WC // 2 + 1):
        forward(k)
    adam(0)
    for k in range(WC // 2 + 1, WC):
        forward(k)
    for k in range(WC // 2):
        w_y(k).wait_recv()
        w_g(k).start()
    adam(1)
    st_one = pltpu.make_async_copy(m_one, first_out, store_sem.at[0])
    st_two = pltpu.make_async_copy(m_two, second_out, store_sem.at[1])
    st_one.start()
    st_two.start()
    b_x.wait_recv()
    b_y.start()
    b_f.start()
    for k in range(WC // 2, WC):
        w_y(k).wait_recv()
        w_g(k).start()
    b_y.wait_recv()
    b_g.start()
    for r in range(RC):
        d_x(r).wait_recv()
        d_f(r).start()

    for r in range(RC):
        pc(r).wait_send()
        px(r).wait_send()
        pf(r).wait_send()
        for d in range(1, n_dp):
            rs(r, d).wait_send()
        d_x(r).wait_send()
        d_c(r).wait()
        d_own(r).wait()
        d_f(r).wait()
    for k in range(WC):
        w_x(k).wait_send()
        w_y(k).wait_send()
        w_f(k).wait()
        w_g(k).wait()
    w_core.wait()
    own_w.wait()
    own_b.wait()
    b_core.wait()
    b_x.wait_send()
    b_y.wait_send()
    b_f.wait()
    b_g.wait()
    st_one.wait()
    st_two.wait()


def exchange(n_dp, tokens, out_grad, basis, weights, moment_one, moment_two):
    tokens_own, depth = tokens.shape
    width = out_grad.shape[1]
    rank = basis.shape[1]
    rc = rank // RC
    hidden = weights.shape[1]
    wide = weights.shape[2]
    half = tokens_own // 2
    dma = pltpu.SemaphoreType.DMA
    any_spec = pl.BlockSpec(memory_space=pl.ANY)
    pair = [dma((RC,)), dma((RC,))]
    one = [dma((1,)), dma((1,))]
    many = [dma((WC,)), dma((WC,))]
    return pl.pallas_call(
        functools.partial(exchange_kernel, n_dp),
        name="exchange",
        out_shape=(
            jax.ShapeDtypeStruct(moment_one.shape, f32),
            jax.ShapeDtypeStruct(moment_two.shape, f32),
            jax.ShapeDtypeStruct((4, hidden, rank), bf16),
            jax.ShapeDtypeStruct((4, depth, rank), bf16),
            jax.ShapeDtypeStruct((4, hidden, wide), bf16),
        ),
        in_specs=[any_spec] * 6,
        out_specs=(any_spec,) * 5,
        scratch_shapes=[
            pltpu.VMEM((tokens_own, depth), bf16),
            pltpu.VMEM((depth, rank), bf16),
            pltpu.VMEM((tokens_own, width), bf16),
            pltpu.VMEM((half, rc), f32),
            pltpu.VMEM((RC, half, rc), bf16),
            pltpu.VMEM((RC, half, rc), bf16),
            pltpu.VMEM((RC, half, rc), bf16),
            pltpu.VMEM((RC, half, rc), bf16),
            pltpu.VMEM((RC, tokens_own, rc), bf16),
            pltpu.VMEM((RC, width, rc), bf16),
            pltpu.VMEM((n_dp - 1, RC, hidden, rc), bf16),
            pltpu.VMEM((1, hidden, rank), f32),
            pltpu.VMEM((1, hidden, rank), f32),
            pltpu.VMEM((RC, hidden, rc), bf16),
            dma((5,)),
            dma((4 + RC,)),
            *pair, *pair, *pair,
            dma((RC, n_dp - 1)), dma((RC, n_dp - 1)),
            *pair, *pair, *pair,
            *one, *one, *one, *one, *one,
            *one, *many, *many, *many, *many,
        ],
        compiler_params=pltpu.CompilerParams(
            collective_id=0, has_side_effects=True, vmem_limit_bytes=56 * 2**20
        ),
    )(tokens, out_grad, basis, weights, moment_one, moment_two)


def update_kernel(weights, direction, basis, out):
    delta = lax.dot_general(
        direction[0], basis[0], (((1,), (1,)), ((), ())), preferred_element_type=f32
    )
    out[0] = (weights[0].astype(f32) - step_size * delta).astype(bf16)


def update(walls, dirs, bases):
    blocks, hidden, wide = walls.shape
    parts, depth, rank = bases.shape
    return pl.pallas_call(
        update_kernel,
        name="update",
        grid=(blocks, parts),
        out_shape=jax.ShapeDtypeStruct(walls.shape, bf16),
        in_specs=[
            pl.BlockSpec((1, hidden, depth), lambda i, j: (i, 0, j)),
            pl.BlockSpec((1, hidden, rank), lambda i, j: (i, 0, 0)),
            pl.BlockSpec((1, depth, rank), lambda i, j: (j, 0, 0)),
        ],
        out_specs=pl.BlockSpec((1, hidden, depth), lambda i, j: (i, 0, j)),
        compiler_params=pltpu.CompilerParams(vmem_limit_bytes=40 * 2**20),
    )(walls, dirs, bases)


def shards_kernel(n_dp, tokens, out_grad, subspace_basis, weights, moment_first, moment_second):
    first_new, second_new, dirs, bases, walls = exchange(
        n_dp, tokens, out_grad, subspace_basis, weights, moment_first, moment_second)
    return (update(walls, dirs, bases), first_new, second_new)


def shards(tokens, out_grad, subspace_basis, weights, moment_first, moment_second):
    partial_value = jnp.dot(tokens, subspace_basis, preferred_element_type=jnp.float32)
    projected = lax.psum(partial_value.astype(jnp.bfloat16), "mp")
    subspace = lax.psum_scatter(
        lax.dot_general(
            out_grad, projected, (((0,), (0,)), ((), ())), preferred_element_type=jnp.float32
        ).astype(jnp.bfloat16),
        "dp",
        scatter_dimension=0,
        tiled=True,
    ).astype(jnp.float32)
    gradient = subspace[None]
    first_new = beta_one * moment_first + (1.0 - beta_one) * gradient
    second_new = beta_two * moment_second + (1.0 - beta_two) * gradient * gradient
    direction = (
        first_new / correction_one / (jnp.sqrt(second_new / correction_two) + epsilon)
    ).astype(jnp.bfloat16)
    weight_delta = lax.dot_general(
        direction[0],
        lax.all_gather(subspace_basis, "mp", axis=0, tiled=True),
        (((1,), (1,)), ((), ())),
        preferred_element_type=jnp.float32,
    )
    updated = (weights[0].astype(jnp.float32) - step_size * weight_delta).astype(jnp.bfloat16)
    result = lax.all_gather(updated[None], "mp", axis=0, tiled=True)
    return (result, first_new, second_new)


def solution(mesh):
    if mesh.shape["mp"] == 4 and mesh.shape["grp"] == 2 and mesh.shape["dp"] == 4:
        body = functools.partial(shards_kernel, mesh.shape["dp"])
    else:
        body = shards
    return jax.shard_map(
        body,
        mesh=mesh,
        in_specs=(
            P(("grp", "dp"), "mp"),
            P(("grp", "dp"), "mp"),
            P("mp", None),
            P("mp", "dp", None),
            P("mp", ("grp", "dp"), None),
            P("mp", ("grp", "dp"), None),
        ),
        out_specs=(
            P(None, ("grp", "dp"), None),
            P("mp", ("grp", "dp"), None),
            P("mp", ("grp", "dp"), None),
        ),
        check_vma=False,
    )
```

```python
import functools

import jax
import jax.numpy as jnp
from jax import lax
from jax.experimental import pallas as pl
from jax.experimental.pallas import tpu as pltpu
from jax.sharding import PartitionSpec as P

beta_one = 0.9
beta_two = 0.999
correction_one = 1.0 - 0.9**10
correction_two = 1.0 - 0.999**10
epsilon = 1e-08
step_size = 0.02

MESH = pl.DeviceIdType.MESH
bf16 = jnp.bfloat16
f32 = jnp.float32

RC = 2
WC = 8
UC = 8


def exchange_kernel(
    n_dp,
    tokens, out_grad, basis, weights, moment_one, moment_two,
    first_out, second_out, dirs, bases, walls,
    tok_v, bas_v, bas_t, og_v, p_own, p_send, p_recv, s_send, s_recv, proj,
    g_send, g_recv, m_one, m_two, direction, w_v, bas_all,
    load_sem, store_sem,
    pc_s, pc_r, px_s, px_r, pf_s, pf_r, rs_s, rs_r,
    dc_s, dc_r, dx_s, dx_r, df_s, df_r,
    bc_s, bc_r, bx_s, bx_r, by_s, by_r, bf_s, bf_r, bg_s, bg_r,
    bz_s, bz_r, uo, uc_s, uc_r, wx_s, wx_r, wy_s, wy_r, wf_s, wf_r, wg_s, wg_r,
):
    grp = lax.axis_index("grp")
    dp = lax.axis_index("dp")
    mp = lax.axis_index("mp")
    core = mp % 2
    mate = mp + 1 - 2 * core
    across = mp + 2 - 4 * (mp // 2)
    to_core = {"mp": mate}
    to_x = {"mp": across}
    to_y = {"grp": 1 - grp}

    tokens_own, depth = tokens.shape
    half = tokens_own // 2
    rank = basis.shape[1]
    rc = rank // RC
    hidden = weights.shape[1]
    wide = weights.shape[2]
    wh = wide // 2
    wc = wh // WC
    bh = rank // 2
    bs = bh // n_dp

    def remote(src, dst, ss, rs, where):
        return pltpu.make_async_remote_copy(
            src_ref=src, dst_ref=dst, send_sem=ss, recv_sem=rs,
            device_id=where, device_id_type=MESH,
        )

    loads = [
        pltpu.make_async_copy(src, dst, load_sem.at[i])
        for i, (src, dst) in enumerate(
            [(tokens, tok_v), (basis, bas_v), (out_grad, og_v),
             (moment_one, m_one), (moment_two, m_two), (weights.at[0], w_v)]
        )
    ]
    loads[1].start()
    loads[0].start()
    loads[2].start()

    barrier = pltpu.get_barrier_semaphore()
    for where in (to_core, to_x, to_y):
        pl.semaphore_signal(barrier, inc=1, device_id=where, device_id_type=MESH)
    for d in range(1, n_dp):
        pl.semaphore_signal(
            barrier, inc=1, device_id={"dp": (dp + d) % n_dp}, device_id_type=MESH
        )
    pl.semaphore_wait(barrier, 3 + n_dp - 1)

    def w_cols(side, k):
        return pl.ds(side * wh + k * wc, wc)

    def w_x(k):
        return remote(weights.at[0, :, w_cols(grp, k)], walls.at[mp, :, w_cols(grp, k)],
                      wx_s.at[k], wx_r.at[k], to_x)

    def w_y(k):
        view = walls.at[across, :, w_cols(grp, k)]
        return remote(view, view, wy_s.at[k], wy_r.at[k], to_y)

    def w_f(k):
        view = walls.at[across, :, w_cols(grp, k)]
        return remote(view, view, wf_s.at[k], wf_r.at[k], to_core)

    def w_g(k):
        view = walls.at[across, :, w_cols(1 - grp, k)]
        return remote(view, view, wg_s.at[k], wg_r.at[k], to_core)

    def project(r, row, dst):
        def body(i, _):
            at = pl.multiple_of(row + i * 256, 256)
            dst[pl.ds(pl.multiple_of(i * 256, 256), 256), :] = jnp.dot(
                tok_v[pl.ds(at, 256), :], bas_v[:, r * rc:(r + 1) * rc],
                preferred_element_type=f32,
            ).astype(dst.dtype)
            return 0
        lax.fori_loop(0, half // 256, body, 0)

    def pc(r):
        return remote(p_send.at[r], p_recv.at[r], pc_s.at[r], pc_r.at[r], to_core)

    def px(r):
        return remote(s_send.at[r], s_recv.at[r], px_s.at[r], px_r.at[r], to_x)

    def pf(r):
        view = proj.at[r, pl.ds(core * half, half), :]
        return remote(view, view, pf_s.at[r], pf_r.at[r], to_core)

    loads[1].wait()
    def turn(i, _):
        at = pl.multiple_of(i * 128, 128)
        bas_t[:, pl.ds(at, 128)] = bas_v[pl.ds(at, 128), :].T
        return 0
    lax.fori_loop(0, depth // 128, turn, 0)
    own_b = pltpu.make_async_copy(bas_t, bases.at[mp], store_sem.at[2])
    own_b.start()
    b_core = remote(bas_t, bases.at[mp], bc_s.at[0], bc_r.at[0], to_core)
    b_core.start()
    rows_piece = pl.ds(grp * bh + dp * bs, bs)
    rows_mine = pl.ds(grp * bh, bh)
    rows_other = pl.ds((1 - grp) * bh, bh)
    b_x = remote(bas_t.at[rows_piece, :], bases.at[mp, rows_piece, :],
                 bx_s.at[0], bx_r.at[0], to_x)
    b_x.start()
    b_view_piece = bases.at[across, rows_piece, :]
    b_z = [
        remote(b_view_piece, b_view_piece, bz_s.at[d - 1], bz_r.at[d - 1],
               {"dp": (dp + d) % n_dp})
        for d in range(1, n_dp)
    ]
    b_view = bases.at[across, rows_mine, :]
    b_y = remote(b_view, b_view, by_s.at[0], by_r.at[0], to_y)
    b_f = remote(b_view, b_view, bf_s.at[0], bf_r.at[0], to_core)
    b_view_other = bases.at[across, rows_other, :]
    b_g = remote(b_view_other, b_view_other, bg_s.at[0], bg_r.at[0], to_core)

    loads[0].wait()
    for r in range(RC):
        project(r, (1 - core) * half, p_send.at[r])
        pc(r).start()
        project(r, core * half, p_own)
        pc(r).wait_recv()
        s_send[r] = (p_own[...] + p_recv[r].astype(f32)).astype(bf16)
        px(r).start()
        w_x(r).start()
        if r == 0:
            b_x.wait_recv()
            for copy in b_z:
                copy.start()

    for i in (3, 4, 5):
        loads[i].start()

    def forward(k):
        w_x(k).wait_recv()
        w_y(k).start()
        w_f(k).start()

    def rs(r, d):
        to = (dp + d) % n_dp
        return remote(g_send.at[r, pl.ds(to * hidden, hidden), :], g_recv.at[d - 1, r],
                      rs_s.at[r, d - 1], rs_r.at[r, d - 1], {"dp": to})

    width = out_grad.shape[0]
    tile = 256
    full = width // tile

    def gradient(r, at, size):
        g_send[r, pl.ds(at, size), :] = jnp.dot(
            og_v[pl.ds(at, size), :], proj[r], preferred_element_type=f32
        ).astype(bf16)

    for r in range(RC):
        px(r).wait_recv()
        if r == RC - 1:
            for k in range(RC, WC):
                w_x(k).start()
        proj[r, pl.ds(core * half, half), :] = (
            s_send[r].astype(f32) + s_recv[r].astype(f32)
        ).astype(bf16)
        pf(r).start()
        if r == 0:
            loads[2].wait()
        pf(r).wait_recv()

        def body(i, _, r=r):
            gradient(r, pl.multiple_of(i * tile, tile), tile)
            return 0
        lax.fori_loop(0, full, body, 0)
        if width % tile:
            gradient(r, full * tile, width % tile)
        for d in range(n_dp - 1, 0, -1):
            rs(r, d).start()
        if r == 0:
            forward(0)
            for copy in b_z:
                copy.wait_recv()
            b_y.start()
            b_f.start()

    def d_c(r):
        return remote(direction.at[r], dirs.at[mp, :, pl.ds(r * rc, rc)],
                      dc_s.at[r], dc_r.at[r], to_core)

    def d_x(r):
        return remote(direction.at[r], dirs.at[mp, :, pl.ds(r * rc, rc)],
                      dx_s.at[r], dx_r.at[r], to_x)

    def d_f(r):
        view = dirs.at[across, :, pl.ds(r * rc, rc)]
        return remote(view, view, df_s.at[r], df_r.at[r], to_core)

    def d_own(r):
        return pltpu.make_async_copy(
            direction.at[r], dirs.at[mp, :, pl.ds(r * rc, rc)], store_sem.at[4 + r])

    def adam(r):
        for d in range(1, n_dp):
            rs(r, d).wait_recv()
        cols = slice(r * rc, (r + 1) * rc)

        for at in range(0, hidden, 128):
            size = min(128, hidden - at)
            rows = slice(at, at + size)
            own = pl.multiple_of(dp * hidden + at, 16)
            total = g_send[r, pl.ds(own, size), :].astype(f32)
            for d in range(n_dp - 1):
                total = total + g_recv[d, r, rows, :].astype(f32)
            first = beta_one * m_one[0, rows, cols] + (1.0 - beta_one) * total
            second = beta_two * m_two[0, rows, cols] + (1.0 - beta_two) * total * total
            m_one[0, rows, cols] = first
            m_two[0, rows, cols] = second
            direction[r, rows, :] = (
                first / correction_one / (jnp.sqrt(second / correction_two) + epsilon)
            ).astype(bf16)
        d_x(r).start()
        d_c(r).start()
        d_own(r).start()

    for i in (3, 4, 5):
        loads[i].wait()
    for k in range(1, WC // 2):
        forward(k)
    b_y.wait_recv()
    b_g.start()
    adam(0)
    for k in range(WC // 2, WC - 1):
        forward(k)
    for k in range(WC // 2):
        w_y(k).wait_recv()
        w_g(k).start()
    b_core.wait_recv()
    b_f.wait_recv()
    b_g.wait_recv()
    own_b.wait()
    load_b = pltpu.make_async_copy(bases, bas_all, load_sem.at[6])
    load_b.start()
    forward(WC - 1)
    adam(1)
    st_one = pltpu.make_async_copy(m_one, first_out, store_sem.at[0])
    st_two = pltpu.make_async_copy(m_two, second_out, store_sem.at[1])
    st_one.start()
    st_two.start()
    load_b.wait()

    uw = wide // UC

    def u_own(k):
        return pltpu.make_async_copy(
            w_v.at[:, pl.ds(k * uw, uw)], walls.at[mp, :, pl.ds(k * uw, uw)], uo.at[k])

    def u_c(k):
        return remote(w_v.at[:, pl.ds(k * uw, uw)], walls.at[mp, :, pl.ds(k * uw, uw)],
                      uc_s.at[k], uc_r.at[k], to_core)

    def u_step(k):
        block, at = (k * uw) // depth, (k * uw) % depth
        cols = slice(k * uw, (k + 1) * uw)
        delta = jnp.dot(direction[0], bas_all[block, 0:rc, at:at + uw], preferred_element_type=f32)
        for r in range(1, RC):
            delta = delta + jnp.dot(
                direction[r], bas_all[block, r * rc:(r + 1) * rc, at:at + uw],
                preferred_element_type=f32)
        w_v[:, cols] = (w_v[:, cols].astype(f32) - step_size * delta).astype(bf16)
        u_own(k).start()
        u_c(k).start()

    for k in range(UC // 2):
        u_step(k)
    for k in range(WC // 2, WC - 1):
        w_y(k).wait_recv()
        w_g(k).start()
    d_x(0).wait_recv()
    d_f(0).start()
    for k in range(UC // 2, UC):
        u_step(k)
    w_y(WC - 1).wait_recv()
    w_g(WC - 1).start()
    for r in range(1, RC):
        d_x(r).wait_recv()
        d_f(r).start()

    for r in range(RC):
        pc(r).wait_send()
        px(r).wait_send()
        pf(r).wait_send()
        for d in range(1, n_dp):
            rs(r, d).wait_send()
        d_x(r).wait_send()
        d_c(r).wait()
        d_own(r).wait()
        d_f(r).wait()
    for k in range(WC):
        w_x(k).wait_send()
        w_y(k).wait_send()
        w_f(k).wait()
        w_g(k).wait()
    for k in range(UC):
        u_own(k).wait()
        u_c(k).wait()
    b_core.wait_send()
    for copy in b_z:
        copy.wait_send()
    b_x.wait_send()
    b_y.wait_send()
    b_f.wait_send()
    b_g.wait_send()
    st_one.wait()
    st_two.wait()


def exchange(n_dp, tokens, out_grad, basis, weights, moment_one, moment_two):
    tokens_own, depth = tokens.shape
    width = out_grad.shape[0]
    rank = basis.shape[1]
    rc = rank // RC
    hidden = weights.shape[1]
    wide = weights.shape[2]
    half = tokens_own // 2
    dma = pltpu.SemaphoreType.DMA
    any_spec = pl.BlockSpec(memory_space=pl.ANY)
    pair = [dma((RC,)), dma((RC,))]
    one = [dma((1,)), dma((1,))]
    many = [dma((WC,)), dma((WC,))]
    return pl.pallas_call(
        functools.partial(exchange_kernel, n_dp),
        name="exchange",
        out_shape=(
            jax.ShapeDtypeStruct(moment_one.shape, f32),
            jax.ShapeDtypeStruct(moment_two.shape, f32),
            jax.ShapeDtypeStruct((4, hidden, rank), bf16),
            jax.ShapeDtypeStruct((4, rank, depth), bf16),
            jax.ShapeDtypeStruct((4, hidden, wide), bf16),
        ),
        in_specs=[any_spec] * 6,
        out_specs=(any_spec,) * 5,
        scratch_shapes=[
            pltpu.VMEM((tokens_own, depth), bf16),
            pltpu.VMEM((depth, rank), bf16),
            pltpu.VMEM((rank, depth), bf16),
            pltpu.VMEM((width, tokens_own), bf16),
            pltpu.VMEM((half, rc), f32),
            pltpu.VMEM((RC, half, rc), bf16),
            pltpu.VMEM((RC, half, rc), bf16),
            pltpu.VMEM((RC, half, rc), bf16),
            pltpu.VMEM((RC, half, rc), bf16),
            pltpu.VMEM((RC, tokens_own, rc), bf16),
            pltpu.VMEM((RC, width, rc), bf16),
            pltpu.VMEM((n_dp - 1, RC, hidden, rc), bf16),
            pltpu.VMEM((1, hidden, rank), f32),
            pltpu.VMEM((1, hidden, rank), f32),
            pltpu.VMEM((RC, hidden, rc), bf16),
            pltpu.VMEM((hidden, wide), bf16),
            pltpu.VMEM((4, rank, depth), bf16),
            dma((7,)),
            dma((4 + RC,)),
            *pair, *pair, *pair,
            dma((RC, n_dp - 1)), dma((RC, n_dp - 1)),
            *pair, *pair, *pair,
            *one, *one, *one, *one, *one,
            dma((n_dp - 1,)), dma((n_dp - 1,)), dma((UC,)), dma((UC,)), dma((UC,)),
            *many, *many, *many, *many,
        ],
        compiler_params=pltpu.CompilerParams(
            collective_id=0, has_side_effects=True, vmem_limit_bytes=58 * 2**20
        ),
    )(tokens, out_grad, basis, weights, moment_one, moment_two)


def update_kernel(
    walls, dirs, bases, first, second, out, first_out, second_out,
    w_v, d_v, b_v, m_v, d_sem, b_sem, m_in, m_out, w_in, w_out,
):
    base = 2 * (lax.axis_index("mp") // 2)
    hidden, wide = walls.shape[1:]
    parts, _, depth = bases.shape
    where = (2 - base, 3 - base, base, base + 1)
    cuts = [hidden * i // parts // 16 * 16 for i in range(parts)] + [hidden]

    def piece(slot, p):
        if slot < 2:
            return (slice(None), pl.ds(p * depth, depth))
        return (pl.ds(cuts[p], cuts[p + 1] - cuts[p]), slice(None))

    def fetch(slot, p):
        at = piece(slot, p)
        return pltpu.make_async_copy(
            walls.at[(where[slot],) + at], w_v.at[(slot,) + at], w_in.at[slot, p])

    def put(slot, p):
        at = piece(slot, p)
        return pltpu.make_async_copy(
            w_v.at[(slot,) + at], out.at[(where[slot],) + at], w_out.at[slot, p])

    fetch_d = [pltpu.make_async_copy(dirs.at[where[i]], d_v.at[i], d_sem.at[i]) for i in range(2)]
    fetch_b = [pltpu.make_async_copy(bases.at[p], b_v.at[p], b_sem.at[p]) for p in range(parts)]
    fetch_m = [pltpu.make_async_copy(first, m_v.at[0], m_in.at[0]),
               pltpu.make_async_copy(second, m_v.at[1], m_in.at[1])]
    put_m = [pltpu.make_async_copy(m_v.at[0], first_out, m_out.at[0]),
             pltpu.make_async_copy(m_v.at[1], second_out, m_out.at[1])]
    fetch_d[0].start()
    for p in range(parts):
        fetch_b[p].start()
        fetch(0, p).start()
        fetch(2, p).start()
    fetch_d[1].start()
    for p in range(parts):
        fetch(1, p).start()
        fetch(3, p).start()
    for copy in fetch_m:
        copy.start()

    for slot in range(2):
        fetch_d[slot].wait()
        for p in range(parts):
            if slot == 0:
                fetch_b[p].wait()
            fetch(slot, p).wait()
            for at in range(0, depth, 512):
                cols = slice(p * depth + at, p * depth + at + 512)
                delta = jnp.dot(d_v[slot], b_v[p, :, at:at + 512], preferred_element_type=f32)
                w_v[slot, :, cols] = (
                    w_v[slot, :, cols].astype(f32) - step_size * delta
                ).astype(bf16)
            put(slot, p).start()
            fetch(slot + 2, p).wait()
            put(slot + 2, p).start()
    for copy_in, copy in zip(fetch_m, put_m):
        copy_in.wait()
        copy.start()
    for slot in range(4):
        for p in range(parts):
            put(slot, p).wait()
    for copy in put_m:
        copy.wait()


def update(walls, dirs, bases, first, second):
    parts, rank, depth = bases.shape
    hidden = walls.shape[1]
    any_spec = pl.BlockSpec(memory_space=pl.ANY)
    dma = pltpu.SemaphoreType.DMA
    return pl.pallas_call(
        update_kernel,
        name="update",
        out_shape=(
            jax.ShapeDtypeStruct(walls.shape, bf16),
            jax.ShapeDtypeStruct(first.shape, f32),
            jax.ShapeDtypeStruct(second.shape, f32),
        ),
        in_specs=[any_spec] * 5,
        out_specs=(any_spec,) * 3,
        scratch_shapes=[
            pltpu.VMEM(walls.shape, bf16),
            pltpu.VMEM((2, hidden, rank), bf16),
            pltpu.VMEM(bases.shape, bf16),
            pltpu.VMEM((2,) + first.shape, f32),
            dma((2,)), dma((parts,)), dma((2,)), dma((2,)),
            dma((4, parts)), dma((4, parts)),
        ],
        compiler_params=pltpu.CompilerParams(vmem_limit_bytes=60 * 2**20),
    )(walls, dirs, bases, first, second)


def shards_kernel(n_dp, tokens, out_grad, subspace_basis, weights, moment_first, moment_second):
    first_new, second_new, dirs, bases, walls = exchange(
        n_dp, tokens, out_grad.T, subspace_basis, weights, moment_first, moment_second)
    return update(walls, dirs, bases, first_new, second_new)


def shards(tokens, out_grad, subspace_basis, weights, moment_first, moment_second):
    partial_value = jnp.dot(tokens, subspace_basis, preferred_element_type=jnp.float32)
    projected = lax.psum(partial_value.astype(jnp.bfloat16), "mp")
    subspace = lax.psum_scatter(
        lax.dot_general(
            out_grad, projected, (((0,), (0,)), ((), ())), preferred_element_type=jnp.float32
        ).astype(jnp.bfloat16),
        "dp",
        scatter_dimension=0,
        tiled=True,
    ).astype(jnp.float32)
    gradient = subspace[None]
    first_new = beta_one * moment_first + (1.0 - beta_one) * gradient
    second_new = beta_two * moment_second + (1.0 - beta_two) * gradient * gradient
    direction = (
        first_new / correction_one / (jnp.sqrt(second_new / correction_two) + epsilon)
    ).astype(jnp.bfloat16)
    weight_delta = lax.dot_general(
        direction[0],
        lax.all_gather(subspace_basis, "mp", axis=0, tiled=True),
        (((1,), (1,)), ((), ())),
        preferred_element_type=jnp.float32,
    )
    updated = (weights[0].astype(jnp.float32) - step_size * weight_delta).astype(jnp.bfloat16)
    result = lax.all_gather(updated[None], "mp", axis=0, tiled=True)
    return (result, first_new, second_new)


def solution(mesh):
    if mesh.shape["mp"] == 4 and mesh.shape["grp"] == 2 and mesh.shape["dp"] == 4:
        body = functools.partial(shards_kernel, mesh.shape["dp"])
    else:
        body = shards
    return jax.shard_map(
        body,
        mesh=mesh,
        in_specs=(
            P(("grp", "dp"), "mp"),
            P(("grp", "dp"), "mp"),
            P("mp", None),
            P("mp", "dp", None),
            P("mp", ("grp", "dp"), None),
            P("mp", ("grp", "dp"), None),
        ),
        out_specs=(
            P(None, ("grp", "dp"), None),
            P("mp", ("grp", "dp"), None),
            P("mp", ("grp", "dp"), None),
        ),
        check_vma=False,
    )
```
